32 devices in a mesh: groups: 2 (over x), dp: 8 (over z, y), mp: 2 (over core).
Axes of the slice: x: 2, y: 2, z: 4, core: 2. Of those that a mesh axis runs over, the one named last changes fastest.
Arguments:
- acts: bfloat16 [6144, 5120], P(('groups', 'dp'), 'mp'), parts along dimension 0, may hold values from -6 to 6
- grads_out: bfloat16 [6144, 27648], P(('groups', 'dp'), 'mp'), parts along dimension 0, may hold values from -6 to 6
- basis_in: bfloat16 [5120, 64], P(('mp', 'dp')), may hold values from -0.078125 to 0.078125
- basis_out: bfloat16 [27648, 64], P(('mp', 'dp')), may hold values from -0.0390625 to 0.0390625
- owner: int32 [768, 1], P(('groups', 'dp')), parts along dimension 0, may hold values from 0 to 7; in each aligned block of 48 rows (0 to 47, 48 to 95, ...) at most 12 rows name the same one
- slot: int32 [768], P(('groups', 'dp')), parts along dimension 0, may hold values from 0 to 1
- fill: int32 [768], P(('groups', 'dp')), parts along dimension 0, may hold values from 1 to 8
Outputs:
- example_grads: float32 [32, 4096], P(('groups', 'dp')), parts along dimension 0
The draws below stay inside these ranges and needn't reach their ends.
There are 2 independent parts, one for each index of `groups`. The reference program is written for one: setup_inputs(seed, part) draws one part's arguments, and reference() takes and returns one part's arrays. A program takes and returns all parts, laid end to end along the dimension named above; an argument that names none is the same for every part. Nothing has to cross between parts.
Inputs may be any that keep to these rules, and one draw needn't show every extreme that they name: Among the blocks of one index of dp, at most 12 name the same owner, a bound that some block reaches of them.
All inputs are finite; a program needn't handle non-finite values.
Results may differ from the reference program's by a relative error of at most 0.0041.
Values may be sent and summed in bfloat16 or wider, within the bound.
A program may use at most 64 MiB of HBM per device.

```python
import math
import jax
import jax.numpy as jnp
import numpy as np
from jax import lax

D = 5120
FF = 27648
RANK = 64
BLK = 8
SLOTS = 2
TOK_DEV = 384
MOST = 12
TOKENS = 3072
BLOCKS = 384
EXAMPLES = 16
N_DP = 8


def draw_fill(key, part):
    key = jax.random.fold_in(key, 7)
    first_key, second_key = jax.random.split(key)
    partial_value = jax.random.randint(first_key, (BLOCKS,), 1, BLK + 1)
    choose = jax.random.randint(second_key, (BLOCKS,), 0, 3)
    result = jnp.where(choose == 0, partial_value, BLK)
    result = jnp.where(jnp.arange(BLOCKS) == 1, 1, result)
    return result.astype(jnp.int32)


def plant(values, rng, smallest, largest):
    dims = values.shape
    place = [jax.random.randint(jax.random.fold_in(rng, axis), (), 0, dims[axis]) for axis in range(len(dims))]
    values = values.at[tuple(place)].set(smallest)
    longest = dims.index(max(dims))
    place[longest] = (place[longest] + 1) % dims[longest]
    return values.at[tuple(place)].set(largest)


def block_levels(own_key, extent, cuts, low, largest):
    level, own = 1.0, jax.random.fold_in(own_key, 6)
    for axis_at, parts in cuts:
        heights = jnp.exp(jax.random.uniform(jax.random.fold_in(own, axis_at), (parts,), jnp.float32, low / len(cuts), largest / len(cuts)))
        level = level * jnp.repeat(heights, extent[axis_at] // parts).reshape([-1 if axis == axis_at else 1 for axis in range(len(extent))])
    return level


def deal_out(rng, own, number, rows, count, top, limit, lean):
    order = jax.random.permutation(rng, count)
    packed, common = shares(count, rows * top, limit, lean, True), shares(count, rows * top, limit, lean, False)
    places = jnp.arange(count)

    def named(lengths, rotation):
        used = int((lengths > 0).sum())
        fixed = max(1, used // 4)
        moved = fixed + (places - fixed + rotation * (used - fixed)) % max(1, count - fixed)
        return jnp.zeros((count,), jnp.int32).at[order[jnp.where(places < fixed, places, moved)]].set(jnp.asarray(lengths, jnp.int32))

    lengths = jnp.where(number % 4 == 0, named(packed, number // 4), named(common, number - number // 4 - 1))
    mixed = jax.random.permutation(jax.random.fold_in(own, 3), count)
    giver, receiver = mixed[0:count // 2 * 2:2], mixed[1:count // 2 * 2:2]
    room = jnp.minimum(lengths[giver] - 1, limit - lengths[receiver]) // 2
    room = jnp.where((giver == order[0]) | (receiver == order[0]) | (lengths[receiver] == 0), 0, jnp.maximum(room, 0))
    moved = jax.random.randint(jax.random.fold_in(own, 4), (count // 2,), 0, 1 << 20) % (room + 1)
    lengths = lengths.at[giver].add(-moved).at[receiver].add(moved)
    members = jnp.searchsorted(jnp.cumsum(lengths), jnp.arange(rows * top), side="right").astype(jnp.int32)
    listing = members.reshape(top, rows).T
    listing = listing[jax.random.permutation(jax.random.fold_in(own, 1), rows)]
    rotation = jax.random.randint(jax.random.fold_in(own, 2), (rows, 1), 0, top)
    return jnp.take_along_axis(listing, (jnp.arange(top)[None, :] + rotation) % top, axis=1)


def shares(amount, total, reach, lean, full):
    loads = [(1 << 20) // math.isqrt(rank ** lean) + 1 for rank in range(1, amount + 1)]
    largest = reach if full else min(reach, max(-(-total // amount), total * loads[0] // sum(loads)))
    least = 1 if total - largest >= amount - 1 else 0
    given, surplus = [largest] + [least] * (amount - 1), total - largest - least * (amount - 1)
    while surplus > 0:
        candidates = [i for i in range(1, amount) if given[i] < largest] or [i for i in range(1, amount) if given[i] < reach]
        whole, remaining = sum([loads[i] for i in candidates]), surplus
        for i in candidates:
            more = min(reach - given[i], max(1, remaining * loads[i] // whole), surplus)
            given[i] = given[i] + more
            surplus = surplus - more
    return np.array(given)


def bell_draw(rng, extent, width, reach, cuts=(), held_as=jnp.bfloat16):
    values = width * jax.random.normal(rng, extent, jnp.float32)
    if cuts:
        values = values * block_levels(rng, extent, cuts, -0.22, 0.18)
    return jnp.clip(values, -reach, reach).astype(held_as)


def setup_inputs(seed: int = 0, part: int = 0) -> dict:
    seeds = jax.random.split(jax.random.key(seed), 8)
    own_keys = jax.random.split(jax.random.fold_in(seeds[7], part), 8)
    acts = bell_draw(own_keys[0], (TOKENS, D), 1.0, 6.0, ((0, 8), (1, 2)))
    grads_out = bell_draw(own_keys[1], (TOKENS, FF), 1.0, 6.0, ((0, 8), (1, 2)))
    basis_in = bell_draw(seeds[2], (D, RANK), D ** -0.5, 0.078125, ((0, 16),))
    basis_out = bell_draw(seeds[3], (FF, RANK), FF ** -0.5, 0.0390625, ((0, 16),))
    owner_keys = jax.random.split(jax.random.fold_in(own_keys[4], 1), BLOCKS // (TOK_DEV // BLK))
    owner_turns = jax.random.permutation(jax.random.fold_in(own_keys[4], 3), BLOCKS // (TOK_DEV // BLK))
    owner = jax.vmap(lambda own, number: deal_out(jax.random.fold_in(own_keys[4], 2), own, number, TOK_DEV // BLK, N_DP, 1, MOST, 2))(owner_keys, owner_turns).reshape((BLOCKS, 1))
    slot = plant(jax.random.randint(own_keys[5], (BLOCKS,), 0, SLOTS), jax.random.fold_in(own_keys[5], 1), 0, SLOTS - 1).astype(jnp.int32)
    fill = draw_fill(jax.random.fold_in(jax.random.fold_in(seeds[7], part), 71), part)
    return dict(acts=acts, grads_out=grads_out, basis_in=basis_in, basis_out=basis_out, owner=owner, slot=slot, fill=fill)


def reference(acts, grads_out, basis_in, basis_out, owner, slot, fill):
    tokens = acts.shape[0]
    blocks = tokens // BLK
    proj_in = jnp.dot(acts, basis_in, preferred_element_type=jnp.float32)
    proj_out = jnp.dot(grads_out, basis_out, preferred_element_type=jnp.float32)
    position = jnp.arange(tokens).reshape(blocks, BLK) % BLK
    live_mask = (position < fill[:, None]).reshape(tokens, 1)
    live_in = jnp.where(live_mask, proj_in, 0.0).astype(jnp.bfloat16)
    live_out = jnp.where(live_mask, proj_out, 0.0).astype(jnp.bfloat16)
    block_in = live_in.astype(jnp.float32).reshape(blocks, BLK, RANK)
    block_out = live_out.astype(jnp.float32).reshape(blocks, BLK, RANK)
    outer_prod = jnp.einsum('kti,ktj->kij', block_in, block_out, precision=lax.Precision.HIGHEST)
    outer_prod = outer_prod.reshape(blocks, RANK * RANK)
    example = owner[:, 0] * SLOTS + slot
    onehot = (example[:, None] == jnp.arange(EXAMPLES)[None, :]).astype(jnp.float32)
    grad_sum = jnp.dot(onehot.T, outer_prod, precision=lax.Precision.HIGHEST)
    token_count = jnp.dot(onehot.T, fill.astype(jnp.float32), precision=lax.Precision.HIGHEST)
    return grad_sum / jnp.sqrt(jnp.maximum(token_count, 1.0))[:, None]
```

```python
import functools

import jax
import jax.numpy as jnp
from jax import lax
from jax.experimental import pallas as pl
from jax.experimental.pallas import tpu as pltpu
from jax.sharding import PartitionSpec as P

BLK = 8
SLOTS = 2
LANE = 128
ROW_TILE = 16
LOADS = 8
MESH = pl.DeviceIdType.MESH


def dp_at(pos, n):
    back = pos // (n // 2)
    return (1 - back) * (2 * pos) + back * (2 * (n - 1 - pos) + 1)


def place_of(dev, n):
    odd = dev % 2
    return (1 - odd) * (dev // 2) + odd * (n - 1 - dev // 2)


def padded(rows, n):
    spill = max((rows * d) % LANE for d in range(n))
    return -(-(rows + spill) // LANE) * LANE


def start_and_shift(dev, rows, span, total, n):
    offset = dev * rows
    start = offset - offset % LANE
    if any(rows * d - (rows * d) % LANE + span > total for d in range(n)):
        start = jnp.minimum(start, total - span)
    return pl.multiple_of(start, LANE), pl.multiple_of(offset - start, ROW_TILE)


def kernel(
    n, acts_hbm, grads_hbm, basis_in, basis_out, owner, slot, fill, out_ref,
    acts, grads, shards, buf_in, buf_out, acc_in, acc_out, part, other_part, turned,
    message, arrived, half, other_half,
    load_sem, ring_send, ring_recv, x_send, x_recv, mp_send, mp_recv, rs_send, rs_recv,
):
    group, me, core = lax.axis_index("groups"), lax.axis_index("dp"), lax.axis_index("mp")
    tokens = acts.shape[0]
    rows_in, rows_out = basis_in.shape[0], basis_out.shape[0]
    rows = (rows_in + rows_out) // 2
    steps = n // 2
    width = basis_in.shape[1]
    pos = place_of(me, n)
    right = dp_at((pos + 1) % n, n)
    left = dp_at((pos + n - 1) % n, n)
    mate = group + 1 - 2 * (group % 2)
    twin = 1 - core
    to_mate = {"groups": mate}
    to_twin = {"mp": twin}

    loads = []
    slab = tokens // LOADS
    for i in range(LOADS):
        at = pl.ds(i * slab, slab)
        loads.append(pltpu.make_async_copy(grads_hbm.at[at], grads.at[at], load_sem.at[i]))
    loads.append(pltpu.make_async_copy(acts_hbm, acts, load_sem.at[LOADS]))

    barrier = pltpu.get_barrier_semaphore()
    for k in range(1, n):
        pl.semaphore_signal(barrier, inc=1, device_id={"dp": (me + k) % n}, device_id_type=MESH)
    pl.semaphore_signal(barrier, inc=1, device_id=to_mate, device_id_type=MESH)
    pl.semaphore_signal(barrier, inc=1, device_id=to_twin, device_id_type=MESH)

    head = rows - rows_in
    both = jnp.concatenate([basis_in[...], basis_out[pl.ds(0, head), :]], axis=0)
    shards[me] = jnp.concatenate([both, basis_out[pl.ds(head, rows), :]], axis=1)
    pl.semaphore_wait(barrier, n + 1)

    third = (rows // 3) // ROW_TILE * ROW_TILE
    mine_at = (group % 2) * third
    mate_at = (1 - group % 2) * third
    rest = rows - 2 * third
    cut_own = third // 2 // ROW_TILE * ROW_TILE
    cut_rest = rest // 2 // ROW_TILE * ROW_TILE

    def span(base, size, cut, step, way):
        if step < steps:
            return pl.ds(pl.multiple_of(base, ROW_TILE), size)
        if way == 0:
            return pl.ds(pl.multiple_of(base, ROW_TILE), cut)
        return pl.ds(pl.multiple_of(base + cut, ROW_TILE), size - cut)

    def ring_rows(step, way, piece):
        if piece == 0:
            return span(mine_at, third, cut_own, step, way)
        return span(2 * third, rest, cut_rest, step, way)

    def origin(step, way):
        return dp_at((pos + n - step) % n if way == 0 else (pos + step) % n, n)

    def ring_copy(step, way, piece, from_dev):
        ref = shards.at[from_dev, ring_rows(step, way, piece)]
        return pltpu.make_async_remote_copy(
            src_ref=ref, dst_ref=ref,
            send_sem=ring_send.at[way, step - 1, piece],
            recv_sem=ring_recv.at[way, step - 1, piece],
            device_id={"dp": right if way == 0 else left}, device_id_type=MESH,
        )

    def x_copy(step, way, base):
        ref = shards.at[origin(step, way), span(base, third, cut_own, step, way)]
        return pltpu.make_async_remote_copy(
            src_ref=ref, dst_ref=ref,
            send_sem=x_send.at[way, step - 1], recv_sem=x_recv.at[way, step - 1],
            device_id=to_mate, device_id_type=MESH,
        )

    sent = []

    def send(copy):
        copy.start()
        sent.append(copy)

    for piece in range(2):
        for way in range(2):
            send(ring_copy(1, way, piece, me))
    for load in loads:
        load.start()

    acc_in[...] = jnp.zeros_like(acc_in)
    acc_out[...] = jnp.zeros_like(acc_out)
    span_in, span_out = buf_in.shape[0], buf_out.shape[0]

    def multiply(dev):
        start_in, shift_in = start_and_shift(dev, rows_in, span_in, acts.shape[1], n)
        start_out, shift_out = start_and_shift(dev, rows_out, span_out, grads.shape[1], n)
        buf_in[...] = jnp.zeros_like(buf_in)
        buf_out[...] = jnp.zeros_like(buf_out)
        buf_in[pl.ds(shift_in, rows_in), :] = shards[dev, pl.ds(0, rows_in), :]
        buf_out[pl.ds(shift_out, head), :] = shards[dev, pl.ds(rows_in, head), :]
        packed = shards[dev]
        buf_out[pl.ds(pl.multiple_of(shift_out + head, ROW_TILE), rows), :] = jnp.concatenate(
            [packed[:, width:], packed[:, :width]], axis=1
        )
        acc_in[...] += jnp.dot(
            acts[:, pl.ds(start_in, span_in)], buf_in[...], preferred_element_type=jnp.float32
        )
        acc_out[...] += jnp.dot(
            grads[:, pl.ds(start_out, span_out)], buf_out[...], preferred_element_type=jnp.float32
        )

    def multiply_both(step):
        def body(way, carry):
            multiply(dp_at((pos + (1 - way) * (n - step) + way * step) % n, n))
            return carry
        lax.fori_loop(0, 2, body, 0)

    for load in loads:
        load.wait()
    multiply(me)
    for step in range(1, steps + 1):
        for piece in range(2):
            for way in range(2):
                from_dev = origin(step, way)
                ring_copy(step, way, piece, from_dev).wait_recv()
                if step < steps:
                    send(ring_copy(step + 1, way, piece, from_dev))
                if piece == 0:
                    send(x_copy(step, way, mine_at))
        if step > 1:
            for way in range(2):
                x_copy(step - 1, way, mate_at).wait_recv()
            multiply_both(step - 1)
    for way in range(2):
        x_copy(steps, way, mate_at).wait_recv()
    multiply(origin(steps, 0))

    lane = lax.broadcasted_iota(jnp.int32, (tokens, LANE), 1)
    part[...] = jnp.where(lane < width, acc_in[...], pltpu.roll(acc_out[...], width, 1))
    swap = pltpu.make_async_remote_copy(
        src_ref=part, dst_ref=other_part, send_sem=mp_send.at[0], recv_sem=mp_recv.at[0],
        device_id=to_twin, device_id_type=MESH,
    )
    swap.start()

    blocks = owner.shape[0]
    examples = n * SLOTS
    eye = lax.broadcasted_iota(jnp.int32, (blocks, blocks), 0) == lax.broadcasted_iota(
        jnp.int32, (blocks, blocks), 1
    )
    owner_row = jnp.sum(jnp.where(eye, owner[...], 0), axis=0, keepdims=True)
    example = (owner_row * SLOTS + slot[...]).astype(jnp.float32)
    facts = jnp.concatenate(
        [jnp.broadcast_to(example, (8, blocks)), jnp.broadcast_to(fill[...].astype(jnp.float32), (8, blocks))],
        axis=0,
    ).astype(jnp.bfloat16)
    token_at = lax.broadcasted_iota(jnp.int32, (blocks, tokens), 1)
    spread = (token_at // BLK == lax.broadcasted_iota(jnp.int32, (blocks, tokens), 0)).astype(jnp.float32)
    by_token = jnp.dot(facts, spread.astype(jnp.bfloat16), preferred_element_type=jnp.float32)
    place = lax.broadcasted_iota(jnp.int32, (1, tokens), 1) % BLK
    live = place.astype(jnp.float32) < by_token[8:9, :]
    number = lax.broadcasted_iota(jnp.int32, (examples, tokens), 0).astype(jnp.float32)
    weight = jnp.where((number == by_token[0:1, :]) & live, 1.0, 0.0)
    count = jnp.broadcast_to(jnp.sum(weight, axis=1, keepdims=True), (examples, LANE))

    swap.wait()
    total = part[...] + other_part[...]
    outs = jnp.where(lane < width, pltpu.roll(total, width, 1), total).astype(jnp.bfloat16)
    flipped = jnp.transpose(total)[:width, :]
    quarter = width // 4
    lots = tokens // LANE
    for b in range(lots):
        turned[pl.ds(b * width, width), :] = flipped[:, b * LANE : (b + 1) * LANE]

    def features(first):
        at = core * (width // 2) + first
        return jnp.concatenate(
            [turned[pl.ds(b * width + at, quarter, stride=2), :] for b in range(lots)], axis=1
        )

    evens, odds = features(0), features(1)
    masked = [(evens * weight[e : e + 1, :]).astype(jnp.bfloat16) for e in range(examples)]
    masked += [(odds * weight[e : e + 1, :]).astype(jnp.bfloat16) for e in range(examples)]
    outer = jnp.dot(jnp.concatenate(masked, axis=0), outs, preferred_element_type=jnp.float32)
    size = examples * quarter
    lane_out = lax.broadcasted_iota(jnp.int32, (size, LANE), 1)
    outer = jnp.where(lane_out < width, outer[:size], outer[size:]).astype(jnp.bfloat16)
    data = SLOTS * quarter
    for d in range(n):
        message[d, pl.ds(0, data), :] = outer[d * data : (d + 1) * data]
        message[d, pl.ds(data, 8 * SLOTS), :] = jnp.concatenate(
            [jnp.broadcast_to(count[d * SLOTS + s : d * SLOTS + s + 1, :], (8, LANE)) for s in range(SLOTS)],
            axis=0,
        ).astype(jnp.bfloat16)

    def route(k, slot_at):
        peer = (me + k) % n
        return pltpu.make_async_remote_copy(
            src_ref=message.at[peer], dst_ref=arrived.at[slot_at],
            send_sem=rs_send.at[k - 1], recv_sem=rs_recv.at[k - 1],
            device_id={"dp": peer}, device_id_type=MESH,
        )

    for k in range(1, n):
        send(route(k, me))
    summed = message[me].astype(jnp.float32)
    for k in range(1, n):
        source = (me + n - k) % n
        route(k, source).wait_recv()
        summed = summed + arrived[source].astype(jnp.float32)
    scale = [
        jnp.broadcast_to(
            jnp.sqrt(jnp.maximum(summed[data + 8 * s : data + 8 * s + 1, :], 1.0)), (quarter, LANE)
        )
        for s in range(SLOTS)
    ]
    half[...] = summed[:data] / jnp.concatenate(scale, axis=0)
    last = pltpu.make_async_remote_copy(
        src_ref=half, dst_ref=other_half, send_sem=mp_send.at[1], recv_sem=mp_recv.at[1],
        device_id=to_twin, device_id_type=MESH,
    )
    last.start()
    for copy in sent:
        copy.wait_send()
    last.wait()
    for s in range(SLOTS):
        at = pl.ds(s * quarter, quarter)
        out_ref[s, pl.ds(pl.multiple_of(core * quarter, 8), quarter), :] = half[at, :]
        out_ref[s, pl.ds(pl.multiple_of(twin * quarter, 8), quarter), :] = other_half[at, :]


def local(acts, grads_out, basis_in, basis_out, owner, slot, fill):
    n = lax.axis_size("dp")
    tokens = acts.shape[0]
    width = basis_in.shape[1]
    rows = (basis_in.shape[0] + basis_out.shape[0]) // 2
    steps = n // 2
    span_in, span_out = padded(basis_in.shape[0], n), padded(basis_out.shape[0], n)
    quarter = width // 4
    message_rows = SLOTS * quarter + 8 * SLOTS
    f32, bf16 = jnp.float32, jnp.bfloat16
    vmem = pl.BlockSpec(memory_space=pltpu.VMEM)
    hbm = pl.BlockSpec(memory_space=pl.ANY)
    dma = pltpu.SemaphoreType.DMA
    result = pl.pallas_call(
        functools.partial(kernel, n),
        out_shape=jax.ShapeDtypeStruct((SLOTS, width // 2, LANE), f32),
        in_specs=[hbm, hbm, vmem, vmem, vmem, vmem, vmem],
        out_specs=vmem,
        scratch_shapes=[
            pltpu.VMEM(acts.shape, bf16),
            pltpu.VMEM(grads_out.shape, bf16),
            pltpu.VMEM((n, rows, LANE), bf16),
            pltpu.VMEM((span_in, LANE), bf16),
            pltpu.VMEM((span_out, LANE), bf16),
            pltpu.VMEM((tokens, LANE), f32),
            pltpu.VMEM((tokens, LANE), f32),
            pltpu.VMEM((tokens, LANE), f32),
            pltpu.VMEM((tokens, LANE), f32),
            pltpu.VMEM((width * (tokens // LANE), LANE), f32),
            pltpu.VMEM((n, message_rows, LANE), bf16),
            pltpu.VMEM((n, message_rows, LANE), bf16),
            pltpu.VMEM((SLOTS * quarter, LANE), f32),
            pltpu.VMEM((SLOTS * quarter, LANE), f32),
            dma((LOADS + 1,)),
            dma((2, steps, 2)),
            dma((2, steps, 2)),
            dma((2, steps)),
            dma((2, steps)),
            dma((2,)),
            dma((2,)),
            dma((n - 1,)),
            dma((n - 1,)),
        ],
        compiler_params=pltpu.CompilerParams(
            collective_id=0, has_side_effects=True, vmem_limit_bytes=40 * 1024 * 1024
        ),
    )(acts, grads_out, basis_in, basis_out, owner, slot[None, :], fill[None, :])
    return result.reshape(SLOTS, width * width)


def solution(mesh):
    return jax.shard_map(
        local,
        mesh=mesh,
        in_specs=(
            P(("groups", "dp"), "mp"),
            P(("groups", "dp"), "mp"),
            P(("mp", "dp"), None),
            P(("mp", "dp"), None),
            P(("groups", "dp"), None),
            P(("groups", "dp")),
            P(("groups", "dp")),
        ),
        out_specs=P(("groups", "dp"), None),
        check_vma=False,
    )
```

```python
import functools

import jax
import jax.numpy as jnp
from jax import lax
from jax.experimental import pallas as pl
from jax.experimental.pallas import tpu as pltpu
from jax.sharding import PartitionSpec as P

BLK = 8
SLOTS = 2
LANE = 128
ROW_TILE = 16
LOADS = 8
MESH = pl.DeviceIdType.MESH


def dp_at(pos, n):
    back = pos // (n // 2)
    return (1 - back) * (2 * pos) + back * (2 * (n - 1 - pos) + 1)


def place_of(dev, n):
    odd = dev % 2
    return (1 - odd) * (dev // 2) + odd * (n - 1 - dev // 2)


def padded(rows, n):
    spill = max((rows * d) % LANE for d in range(n))
    return -(-(rows + spill) // LANE) * LANE


def start_and_shift(dev, rows, span, total, n):
    offset = dev * rows
    start = offset - offset % LANE
    if any(rows * d - (rows * d) % LANE + span > total for d in range(n)):
        start = jnp.minimum(start, total - span)
    return pl.multiple_of(start, LANE), offset - start


def kernel(
    n, acts_hbm, grads_hbm, basis_in_hbm, basis_out_hbm, owner_hbm, slot_hbm, fill_hbm, out_ref,
    acts, grads, basis_in, basis_out, owner, slot, fill, shards, acc_in, acc_out, part, other_part,
    turned, message, arrived, half, other_half,
    load_sem, small_sem, ring_send, ring_recv, x_send, x_recv, mp_send, mp_recv, rs_send, rs_recv,
):
    group, me, core = lax.axis_index("groups"), lax.axis_index("dp"), lax.axis_index("mp")
    tokens = acts.shape[0]
    width, rows_in = basis_in.shape
    rows_out = basis_out.shape[1]
    span_in, span_out = padded(rows_in, n), padded(rows_out, n)
    steps = n // 2
    pos = place_of(me, n)
    right = dp_at((pos + 1) % n, n)
    left = dp_at((pos + n - 1) % n, n)
    mate = group + 1 - 2 * (group % 2)
    twin = 1 - core
    to_mate = {"groups": mate}
    to_twin = {"mp": twin}

    smalls = [
        pltpu.make_async_copy(source, target, small_sem.at[i])
        for i, (source, target) in enumerate(
            [(basis_out_hbm, basis_out), (basis_in_hbm, basis_in), (owner_hbm, owner),
             (slot_hbm, slot), (fill_hbm, fill)]
        )
    ]
    for copy in smalls:
        copy.start()
    loads = [pltpu.make_async_copy(acts_hbm, acts, load_sem.at[LOADS])]
    slab = tokens // LOADS
    for i in range(LOADS):
        at = pl.ds(i * slab, slab)
        loads.append(pltpu.make_async_copy(grads_hbm.at[at], grads.at[at], load_sem.at[i]))
    for load in loads:
        load.start()

    barrier = pltpu.get_barrier_semaphore()
    for k in range(1, n):
        pl.semaphore_signal(barrier, inc=1, device_id={"dp": (me + k) % n}, device_id_type=MESH)
    pl.semaphore_signal(barrier, inc=1, device_id=to_mate, device_id_type=MESH)
    pl.semaphore_signal(barrier, inc=1, device_id=to_twin, device_id_type=MESH)

    def aligned(basis, span, total):
        rows = basis.shape[1]
        _, shift = start_and_shift(me, rows, span, total, n)
        wide = jnp.concatenate(
            [basis[...].astype(jnp.float32), jnp.zeros((width, span - rows), jnp.float32)], axis=1
        )
        return pltpu.roll(wide, shift, 1).astype(jnp.bfloat16)

    for copy in smalls[:2]:
        copy.wait()
    shards[me, :, pl.ds(0, span_in)] = aligned(basis_in, span_in, acts.shape[1])
    shards[me, :, pl.ds(span_in, span_out)] = aligned(basis_out, span_out, grads.shape[1])
    pl.semaphore_wait(barrier, n + 1)

    tiles = (span_in + span_out) // LANE
    third = -(-tiles // 3)
    mine_at, mate_at = (group % 2) * (third * LANE), (1 - group % 2) * (third * LANE)

    def piece_of(from_dev, piece, step, way):
        if piece == 1:
            columns = pl.ds(2 * third * LANE, (tiles - 2 * third) * LANE)
        else:
            columns = pl.ds(pl.multiple_of(mine_at if piece == 0 else mate_at, LANE), third * LANE)
        if step < steps:
            return shards.at[from_dev, :, columns]
        return shards.at[from_dev, pl.ds(way * (width // 2), width // 2), columns]

    def origin(step, way):
        return dp_at((pos + n - step) % n if way == 0 else (pos + step) % n, n)

    def ring_copy(step, way, piece, from_dev):
        ref = piece_of(from_dev, piece, step, way)
        return pltpu.make_async_remote_copy(
            src_ref=ref, dst_ref=ref,
            send_sem=ring_send.at[way, step - 1, piece],
            recv_sem=ring_recv.at[way, step - 1, piece],
            device_id={"dp": right if way == 0 else left}, device_id_type=MESH,
        )

    def x_copy(step, way, piece):
        ref = piece_of(origin(step, way), piece, step, way)
        return pltpu.make_async_remote_copy(
            src_ref=ref, dst_ref=ref,
            send_sem=x_send.at[way, step - 1], recv_sem=x_recv.at[way, step - 1],
            device_id=to_mate, device_id_type=MESH,
        )

    sent = []

    def send(copy):
        copy.start()
        sent.append(copy)

    for piece in range(2):
        for way in range(2):
            send(ring_copy(1, way, piece, me))
    acc_in[...] = jnp.zeros_like(acc_in)
    acc_out[...] = jnp.zeros_like(acc_out)
    across = (((1,), (1,)), ((), ()))

    def multiply(dev):
        start_in, _ = start_and_shift(dev, rows_in, span_in, acts.shape[1], n)
        start_out, _ = start_and_shift(dev, rows_out, span_out, grads.shape[1], n)
        acc_in[...] += lax.dot_general(
            acts[:, pl.ds(start_in, span_in)], shards[dev, :, pl.ds(0, span_in)],
            across, preferred_element_type=jnp.float32,
        )
        acc_out[...] += lax.dot_general(
            grads[:, pl.ds(start_out, span_out)], shards[dev, :, pl.ds(span_in, span_out)],
            across, preferred_element_type=jnp.float32,
        )

    def multiply_both(step):
        def body(way, carry):
            multiply(dp_at((pos + (1 - way) * (n - step) + way * step) % n, n))
            return carry
        lax.fori_loop(0, 2, body, 0)

    for step in range(1, steps):
        for piece in range(2):
            for way in range(2):
                from_dev = origin(step, way)
                ring_copy(step, way, piece, from_dev).wait_recv()
                send(ring_copy(step + 1, way, piece, from_dev))
                if piece == 0:
                    send(x_copy(step, way, 0))
        if step == 1:
            for load in loads:
                load.wait()
            multiply(me)
        else:
            for way in range(2):
                x_copy(step - 1, way, 2).wait_recv()
            multiply_both(step - 1)
    for way in range(2):
        x_copy(steps - 1, way, 2).wait_recv()
        send(ring_copy(steps, way, 2, origin(steps - 1, way)))
    multiply_both(steps - 1)
    for piece in range(3):
        for way in range(2):
            ring_copy(steps, way, piece, origin(steps, way)).wait_recv()
    multiply(origin(steps, 0))

    lane = lax.broadcasted_iota(jnp.int32, (tokens, LANE), 1)
    part[...] = jnp.concatenate([acc_in[...], acc_out[...]], axis=1)
    swap = pltpu.make_async_remote_copy(
        src_ref=part, dst_ref=other_part, send_sem=mp_send.at[0], recv_sem=mp_recv.at[0],
        device_id=to_twin, device_id_type=MESH,
    )
    swap.start()
    for copy in smalls[2:]:
        copy.wait()

    blocks = owner.shape[1]
    examples = n * SLOTS
    example = (owner[...] * SLOTS + slot[...]).astype(jnp.float32)
    facts = jnp.concatenate(
        [jnp.broadcast_to(example, (8, blocks)), jnp.broadcast_to(fill[...].astype(jnp.float32), (8, blocks))],
        axis=0,
    ).astype(jnp.bfloat16)
    token_at = lax.broadcasted_iota(jnp.int32, (blocks, tokens), 1)
    spread = (token_at // BLK == lax.broadcasted_iota(jnp.int32, (blocks, tokens), 0)).astype(jnp.float32)
    by_token = jnp.dot(facts, spread.astype(jnp.bfloat16), preferred_element_type=jnp.float32)
    place = lax.broadcasted_iota(jnp.int32, (1, tokens), 1) % BLK
    live = place.astype(jnp.float32) < by_token[8:9, :]
    number = lax.broadcasted_iota(jnp.int32, (examples, tokens), 0).astype(jnp.float32)
    weight = jnp.where((number == by_token[0:1, :]) & live, 1.0, 0.0)
    count = jnp.broadcast_to(jnp.sum(weight, axis=1, keepdims=True), (examples, LANE))

    swap.wait()
    total = part[...] + other_part[...]
    outs = jnp.where(lane < width, pltpu.roll(total, width, 1), total).astype(jnp.bfloat16)
    flipped = jnp.transpose(total)[:width, :]
    quarter = width // 4
    lots = tokens // LANE
    for b in range(lots):
        turned[pl.ds(b * width, width), :] = flipped[:, b * LANE : (b + 1) * LANE]

    def features(first):
        at = core * (width // 2) + first
        return jnp.concatenate(
            [turned[pl.ds(b * width + at, quarter, stride=2), :] for b in range(lots)], axis=1
        )

    evens, odds = features(0), features(1)
    masked = [(evens * weight[e : e + 1, :]).astype(jnp.bfloat16) for e in range(examples)]
    masked += [(odds * weight[e : e + 1, :]).astype(jnp.bfloat16) for e in range(examples)]
    outer = jnp.dot(jnp.concatenate(masked, axis=0), outs, preferred_element_type=jnp.float32)
    size = examples * quarter
    lane_out = lax.broadcasted_iota(jnp.int32, (size, LANE), 1)
    outer = jnp.where(lane_out < width, outer[:size], outer[size:]).astype(jnp.bfloat16)
    data = SLOTS * quarter
    for d in range(n):
        message[d, pl.ds(0, data), :] = outer[d * data : (d + 1) * data]
        message[d, pl.ds(data, 8 * SLOTS), :] = jnp.concatenate(
            [jnp.broadcast_to(count[d * SLOTS + s : d * SLOTS + s + 1, :], (8, LANE)) for s in range(SLOTS)],
            axis=0,
        ).astype(jnp.bfloat16)

    def route(k, slot_at):
        peer = (me + k) % n
        return pltpu.make_async_remote_copy(
            src_ref=message.at[peer], dst_ref=arrived.at[slot_at],
            send_sem=rs_send.at[k - 1], recv_sem=rs_recv.at[k - 1],
            device_id={"dp": peer}, device_id_type=MESH,
        )

    for k in range(1, n):
        send(route(k, me))
    summed = message[me].astype(jnp.float32)
    for k in range(1, n):
        source = (me + n - k) % n
        route(k, source).wait_recv()
        summed = summed + arrived[source].astype(jnp.float32)
    scale = [
        jnp.broadcast_to(
            jnp.sqrt(jnp.maximum(summed[data + 8 * s : data + 8 * s + 1, :], 1.0)), (quarter, LANE)
        )
        for s in range(SLOTS)
    ]
    half[...] = summed[:data] / jnp.concatenate(scale, axis=0)
    last = pltpu.make_async_remote_copy(
        src_ref=half, dst_ref=other_half, send_sem=mp_send.at[1], recv_sem=mp_recv.at[1],
        device_id=to_twin, device_id_type=MESH,
    )
    last.start()
    for copy in sent:
        copy.wait_send()
    last.wait()
    for s in range(SLOTS):
        at = pl.ds(s * quarter, quarter)
        out_ref[s, pl.ds(pl.multiple_of(core * quarter, 8), quarter), :] = half[at, :]
        out_ref[s, pl.ds(pl.multiple_of(twin * quarter, 8), quarter), :] = other_half[at, :]


def local(acts, grads_out, basis_in, basis_out, owner, slot, fill):
    n = lax.axis_size("dp")
    tokens = acts.shape[0]
    width = basis_in.shape[1]
    steps = n // 2
    span = padded(basis_in.shape[0], n) + padded(basis_out.shape[0], n)
    quarter = width // 4
    message_rows = SLOTS * quarter + 8 * SLOTS
    f32, bf16, i32 = jnp.float32, jnp.bfloat16, jnp.int32
    hbm = pl.BlockSpec(memory_space=pltpu.HBM)
    dma = pltpu.SemaphoreType.DMA
    blocks = (1, owner.shape[0])
    result = pl.pallas_call(
        functools.partial(kernel, n),
        out_shape=jax.ShapeDtypeStruct((SLOTS, width // 2, LANE), f32),
        in_specs=[hbm] * 7,
        out_specs=pl.BlockSpec(memory_space=pltpu.VMEM),
        scratch_shapes=[
            pltpu.VMEM(acts.shape, bf16),
            pltpu.VMEM(grads_out.shape, bf16),
            pltpu.VMEM(basis_in.shape[::-1], bf16),
            pltpu.VMEM(basis_out.shape[::-1], bf16),
            pltpu.VMEM(blocks, i32),
            pltpu.VMEM(blocks, i32),
            pltpu.VMEM(blocks, i32),
            pltpu.VMEM((n, width, span), bf16),
            pltpu.VMEM((tokens, width), f32),
            pltpu.VMEM((tokens, width), f32),
            pltpu.VMEM((tokens, LANE), f32),
            pltpu.VMEM((tokens, LANE), f32),
            pltpu.VMEM((width * (tokens // LANE), LANE), f32),
            pltpu.VMEM((n, message_rows, LANE), bf16),
            pltpu.VMEM((n, message_rows, LANE), bf16),
            pltpu.VMEM((SLOTS * quarter, LANE), f32),
            pltpu.VMEM((SLOTS * quarter, LANE), f32),
            dma((LOADS + 1,)),
            dma((5,)),
            dma((2, steps, 3)),
            dma((2, steps, 3)),
            dma((2, steps - 1)),
            dma((2, steps - 1)),
            dma((2,)),
            dma((2,)),
            dma((n - 1,)),
            dma((n - 1,)),
        ],
        compiler_params=pltpu.CompilerParams(
            collective_id=0, has_side_effects=True, vmem_limit_bytes=63 * 1024 * 1024
        ),
    )(acts, grads_out, basis_in.T, basis_out.T, owner.T, slot[None, :], fill[None, :])
    return result.reshape(SLOTS, width * width)


def solution(mesh):
    return jax.shard_map(
        local,
        mesh=mesh,
        in_specs=(
            P(("groups", "dp"), "mp"),
            P(("groups", "dp"), "mp"),
            P(("mp", "dp"), None),
            P(("mp", "dp"), None),
            P(("groups", "dp"), None),
            P(("groups", "dp")),
            P(("groups", "dp")),
        ),
        out_specs=P(("groups", "dp"), None),
        check_vma=False,
    )
```

```python
import functools

import jax
import jax.numpy as jnp
from jax import lax
from jax.experimental import pallas as pl
from jax.experimental.pallas import tpu as pltpu
from jax.sharding import PartitionSpec as P

BLK = 8
SLOTS = 2
LANE = 128
ROW_TILE = 16
LOADS = 4
CROSS = 2
STAY = 1
MESH = pl.DeviceIdType.MESH


def dp_at(pos, n):
    back = pos // (n // 2)
    return (1 - back) * (2 * pos) + back * (2 * (n - 1 - pos) + 1)


def place_of(dev, n):
    odd = dev % 2
    return (1 - odd) * (dev // 2) + odd * (n - 1 - dev // 2)


def padded(rows, n):
    spill = max((rows * d) % LANE for d in range(n))
    return -(-(rows + spill) // LANE) * LANE


def cuts(first, size, parts):
    ends = [first + size * i // parts for i in range(parts + 1)]
    return [(low, high - low) for low, high in zip(ends, ends[1:])]


def start_and_shift(dev, rows, span, total, n):
    offset = dev * rows
    start = offset - offset % LANE
    if any(rows * d - (rows * d) % LANE + span > total for d in range(n)):
        start = jnp.minimum(start, total - span)
    return pl.multiple_of(start, LANE), offset - start


def kernel(
    n, acts_hbm, grads_hbm, basis_in_hbm, basis_out_hbm, owner_hbm, slot_hbm, fill_hbm, out_ref,
    acts, grads, basis_in, basis_out, owner, slot, fill, shards, acc_in, acc_out, part, other_part,
    turned, message, arrived, tally, tally_in, half, other_half,
    load_sem, small_sem, ring_send, ring_recv, x_send, x_recv, mp_send, mp_recv, rs_send, rs_recv,
    tally_send, tally_recv,
):
    group, me, core = lax.axis_index("groups"), lax.axis_index("dp"), lax.axis_index("mp")
    tokens = acts.shape[0]
    width, rows_in = basis_in.shape
    rows_out = basis_out.shape[1]
    span_in, span_out = padded(rows_in, n), padded(rows_out, n)
    steps = n // 2
    pos = place_of(me, n)
    right = dp_at((pos + 1) % n, n)
    left = dp_at((pos + n - 1) % n, n)
    mate = group + 1 - 2 * (group % 2)
    twin = 1 - core
    to_mate = {"groups": mate}
    to_twin = {"mp": twin}

    barrier = pltpu.get_barrier_semaphore()
    for device in ({"dp": right}, {"dp": left}, to_mate, to_twin):
        pl.semaphore_signal(barrier, inc=1, device_id=device, device_id_type=MESH)

    smalls = [
        pltpu.make_async_copy(source, target, small_sem.at[i])
        for i, (source, target) in enumerate(
            [(basis_out_hbm, basis_out), (basis_in_hbm, basis_in), (owner_hbm, owner),
             (slot_hbm, slot), (fill_hbm, fill)]
        )
    ]
    for copy in smalls:
        copy.start()
    loads = [pltpu.make_async_copy(acts_hbm, acts, load_sem.at[LOADS])]
    slab = tokens // LOADS
    for i in range(LOADS):
        at = pl.ds(i * slab, slab)
        loads.append(pltpu.make_async_copy(grads_hbm.at[at], grads.at[at], load_sem.at[i]))
    def aligned(basis, span, total):
        rows = basis.shape[1]
        _, shift = start_and_shift(me, rows, span, total, n)
        wide = jnp.concatenate(
            [basis[...].astype(jnp.float32), jnp.zeros((width, span - rows), jnp.float32)], axis=1
        )
        return pltpu.roll(wide, shift, 1).astype(jnp.bfloat16)

    for copy in smalls[:2]:
        copy.wait()
    share = jnp.concatenate(
        [aligned(basis_in, span_in, acts.shape[1]), aligned(basis_out, span_out, grads.shape[1])], axis=1
    )
    tiles, tiles_in = share.shape[1] // LANE, span_in // LANE
    for i in range(tiles):
        shards[me, i] = share[:, i * LANE : (i + 1) * LANE]
    pl.semaphore_wait(barrier, 4)

    third = max(2, tiles * 3 // 8)
    cross = cuts(0, third, CROSS)
    stay = cuts(2 * third, tiles - 2 * third, STAY)
    mine_at, mate_at = (group % 2) * third, (1 - group % 2) * third

    def piece_of(from_dev, base, piece, step, way):
        first, size = piece
        if step < steps:
            return shards.at[from_dev, pl.ds(base + first, size)]
        return shards.at[from_dev, pl.ds(base + first, size), pl.ds(way * (width // 2), width // 2)]

    def origin(step, way):
        return dp_at((pos + n - step) % n if way == 0 else (pos + step) % n, n)

    def ring_copy(step, way, piece, from_dev):
        base, part_of = (mine_at, cross[piece]) if piece < CROSS else (0, stay[piece - CROSS])
        ref = piece_of(from_dev, base, part_of, step, way)
        return pltpu.make_async_remote_copy(
            src_ref=ref, dst_ref=ref,
            send_sem=ring_send.at[way, step - 1, piece],
            recv_sem=ring_recv.at[way, step - 1, piece],
            device_id={"dp": right if way == 0 else left}, device_id_type=MESH,
        )

    def x_copy(step, way, piece, base):
        ref = piece_of(origin(step, way), base, cross[piece], step, way)
        return pltpu.make_async_remote_copy(
            src_ref=ref, dst_ref=ref,
            send_sem=x_send.at[way, step - 1, piece], recv_sem=x_recv.at[way, step - 1, piece],
            device_id=to_mate, device_id_type=MESH,
        )

    def from_mate(step):
        for way in range(2):
            for piece in range(CROSS):
                x_copy(step, way, piece, mate_at).wait_recv()

    sent = []

    def send(copy):
        copy.start()
        sent.append(copy)

    for piece in range(CROSS + STAY):
        for way in range(2):
            send(ring_copy(1, way, piece, me))
    for load in loads:
        load.start()
    acc_in[...] = jnp.zeros_like(acc_in)
    acc_out[...] = jnp.zeros_like(acc_out)
    across = (((1,), (1,)), ((), ()))

    def features_of(dev, first, end):
        return jnp.concatenate([shards[dev, i] for i in range(first, end)], axis=1)

    def multiply(dev):
        start_in, _ = start_and_shift(dev, rows_in, span_in, acts.shape[1], n)
        start_out, _ = start_and_shift(dev, rows_out, span_out, grads.shape[1], n)
        acc_in[...] += lax.dot_general(
            acts[:, pl.ds(start_in, span_in)], features_of(dev, 0, tiles_in),
            across, preferred_element_type=jnp.float32,
        )
        acc_out[...] += lax.dot_general(
            grads[:, pl.ds(start_out, span_out)], features_of(dev, tiles_in, tiles),
            across, preferred_element_type=jnp.float32,
        )

    def multiply_both(step):
        def body(way, carry):
            multiply(dp_at((pos + (1 - way) * (n - step) + way * step) % n, n))
            return carry
        lax.fori_loop(0, 2, body, 0)

    for copy in smalls[2:]:
        copy.wait()
    blocks = owner.shape[1]
    examples = n * SLOTS
    example = (owner[...] * SLOTS + slot[...]).astype(jnp.float32)
    facts = jnp.concatenate(
        [jnp.broadcast_to(example, (8, blocks)), jnp.broadcast_to(fill[...].astype(jnp.float32), (8, blocks))],
        axis=0,
    ).astype(jnp.bfloat16)
    token_at = lax.broadcasted_iota(jnp.int32, (blocks, tokens), 1)
    spread = (token_at // BLK == lax.broadcasted_iota(jnp.int32, (blocks, tokens), 0)).astype(jnp.float32)
    by_token = jnp.dot(facts, spread.astype(jnp.bfloat16), preferred_element_type=jnp.float32)
    place = lax.broadcasted_iota(jnp.int32, (1, tokens), 1) % BLK
    live = place.astype(jnp.float32) < by_token[8:9, :]
    number = lax.broadcasted_iota(jnp.int32, (examples, tokens), 0).astype(jnp.float32)
    weight = jnp.where((number == by_token[0:1, :]) & live, 1.0, 0.0)
    count = jnp.broadcast_to(jnp.sum(weight, axis=1, keepdims=True), (examples, LANE))
    for d in range(n):
        tally[d] = jnp.concatenate(
            [jnp.broadcast_to(count[d * SLOTS + s : d * SLOTS + s + 1, :], (8, LANE)) for s in range(SLOTS)],
            axis=0,
        ).astype(jnp.bfloat16)

    def tally_copy(step, way, slot_at):
        peer = origin(step, 1 - way)
        return pltpu.make_async_remote_copy(
            src_ref=tally.at[peer], dst_ref=tally_in.at[slot_at],
            send_sem=tally_send.at[way, step - 1], recv_sem=tally_recv.at[way, step - 1],
            device_id={"dp": peer}, device_id_type=MESH,
        )

    def pass_on(step, pieces):
        for piece in pieces:
            for way in range(2):
                from_dev = origin(step, way)
                ring_copy(step, way, piece, from_dev).wait_recv()
                if step < steps:
                    send(ring_copy(step + 1, way, piece, from_dev))
                if piece < CROSS:
                    send(x_copy(step, way, piece, mine_at))

    for step in range(1, steps + 1):
        pass_on(step, range(CROSS))
        if step > 2:
            from_mate(step - 2)
            multiply_both(step - 2)
        pass_on(step, range(CROSS, CROSS + STAY))
        for way in range(2 if step < steps else 1):
            send(tally_copy(step, way, me))
        if step == 1:
            for load in loads:
                load.wait()
            multiply(me)
    from_mate(steps - 1)
    multiply_both(steps - 1)
    from_mate(steps)
    multiply(origin(steps, 0))

    lane = lax.broadcasted_iota(jnp.int32, (tokens, LANE), 1)
    part[...] = jnp.concatenate([acc_in[...], acc_out[...]], axis=1)
    swap = pltpu.make_async_remote_copy(
        src_ref=part, dst_ref=other_part, send_sem=mp_send.at[0], recv_sem=mp_recv.at[0],
        device_id=to_twin, device_id_type=MESH,
    )
    swap.start()
    swap.wait()
    total = part[...] + other_part[...]
    outs = jnp.where(lane < width, pltpu.roll(total, width, 1), total).astype(jnp.bfloat16)
    flipped = jnp.transpose(total)[:width, :]
    quarter = width // 4
    lots = tokens // LANE
    for b in range(lots):
        turned[pl.ds(b * width, width), :] = flipped[:, b * LANE : (b + 1) * LANE]

    def features(first):
        at = core * (width // 2) + first
        return jnp.concatenate(
            [turned[pl.ds(b * width + at, quarter, stride=2), :] for b in range(lots)], axis=1
        )

    evens, odds = features(0), features(1)
    masked = [(evens * weight[e : e + 1, :]).astype(jnp.bfloat16) for e in range(examples)]
    masked += [(odds * weight[e : e + 1, :]).astype(jnp.bfloat16) for e in range(examples)]
    outer = jnp.dot(jnp.concatenate(masked, axis=0), outs, preferred_element_type=jnp.float32)
    size = examples * quarter
    lane_out = lax.broadcasted_iota(jnp.int32, (size, LANE), 1)
    outer = jnp.where(lane_out < width, outer[:size], outer[size:]).astype(jnp.bfloat16)
    data = SLOTS * quarter
    for d in range(n):
        message[d] = outer[d * data : (d + 1) * data]

    def route(k, slot_at):
        peer = (me + k) % n
        return pltpu.make_async_remote_copy(
            src_ref=message.at[peer], dst_ref=arrived.at[slot_at],
            send_sem=rs_send.at[k - 1], recv_sem=rs_recv.at[k - 1],
            device_id={"dp": peer}, device_id_type=MESH,
        )

    for k in range(1, n):
        send(route(k, me))
    summed = message[me].astype(jnp.float32)
    for k in range(1, n):
        source = (me + n - k) % n
        route(k, source).wait_recv()
        summed = summed + arrived[source].astype(jnp.float32)
    counted = tally[me].astype(jnp.float32)
    for step in range(1, steps + 1):
        for way in range(2 if step < steps else 1):
            source = origin(step, way)
            tally_copy(step, way, source).wait_recv()
            counted = counted + tally_in[source].astype(jnp.float32)
    scale = [
        jnp.broadcast_to(jnp.sqrt(jnp.maximum(counted[8 * s : 8 * s + 1, :], 1.0)), (quarter, LANE))
        for s in range(SLOTS)
    ]
    half[...] = summed / jnp.concatenate(scale, axis=0)
    last = pltpu.make_async_remote_copy(
        src_ref=half, dst_ref=other_half, send_sem=mp_send.at[1], recv_sem=mp_recv.at[1],
        device_id=to_twin, device_id_type=MESH,
    )
    last.start()
    for copy in sent:
        copy.wait_send()
    last.wait()
    for s in range(SLOTS):
        at = pl.ds(s * quarter, quarter)
        out_ref[s, pl.ds(pl.multiple_of(core * quarter, 8), quarter), :] = half[at, :]
        out_ref[s, pl.ds(pl.multiple_of(twin * quarter, 8), quarter), :] = other_half[at, :]


def local(acts, grads_out, basis_in, basis_out, owner, slot, fill):
    n = lax.axis_size("dp")
    tokens = acts.shape[0]
    width = basis_in.shape[1]
    steps = n // 2
    span = padded(basis_in.shape[0], n) + padded(basis_out.shape[0], n)
    quarter = width // 4
    message_rows = SLOTS * quarter
    f32, bf16, i32 = jnp.float32, jnp.bfloat16, jnp.int32
    hbm = pl.BlockSpec(memory_space=pltpu.HBM)
    dma = pltpu.SemaphoreType.DMA
    blocks = (1, owner.shape[0])
    result = pl.pallas_call(
        functools.partial(kernel, n),
        out_shape=jax.ShapeDtypeStruct((SLOTS, width // 2, LANE), f32),
        in_specs=[hbm] * 7,
        out_specs=pl.BlockSpec(memory_space=pltpu.VMEM),
        scratch_shapes=[
            pltpu.VMEM(acts.shape, bf16),
            pltpu.VMEM(grads_out.shape, bf16),
            pltpu.VMEM(basis_in.shape[::-1], bf16),
            pltpu.VMEM(basis_out.shape[::-1], bf16),
            pltpu.VMEM(blocks, i32),
            pltpu.VMEM(blocks, i32),
            pltpu.VMEM(blocks, i32),
            pltpu.VMEM((n, span // LANE, width, LANE), bf16),
            pltpu.VMEM((tokens, width), f32),
            pltpu.VMEM((tokens, width), f32),
            pltpu.VMEM((tokens, LANE), f32),
            pltpu.VMEM((tokens, LANE), f32),
            pltpu.VMEM((width * (tokens // LANE), LANE), f32),
            pltpu.VMEM((n, message_rows, LANE), bf16),
            pltpu.VMEM((n, message_rows, LANE), bf16),
            pltpu.VMEM((n, 8 * SLOTS, LANE), bf16),
            pltpu.VMEM((n, 8 * SLOTS, LANE), bf16),
            pltpu.VMEM((SLOTS * quarter, LANE), f32),
            pltpu.VMEM((SLOTS * quarter, LANE), f32),
            dma((LOADS + 1,)),
            dma((5,)),
            dma((2, steps, CROSS + STAY)),
            dma((2, steps, CROSS + STAY)),
            dma((2, steps, CROSS)),
            dma((2, steps, CROSS)),
            dma((2,)),
            dma((2,)),
            dma((n - 1,)),
            dma((n - 1,)),
            dma((2, steps)),
            dma((2, steps)),
        ],
        compiler_params=pltpu.CompilerParams(
            collective_id=0, has_side_effects=True, vmem_limit_bytes=63 * 1024 * 1024
        ),
    )(acts, grads_out, basis_in.T, basis_out.T, owner.T, slot[None, :], fill[None, :])
    return result.reshape(SLOTS, width * width)


def solution(mesh):
    return jax.shard_map(
        local,
        mesh=mesh,
        in_specs=(
            P(("groups", "dp"), "mp"),
            P(("groups", "dp"), "mp"),
            P(("mp", "dp"), None),
            P(("mp", "dp"), None),
            P(("groups", "dp"), None),
            P(("groups", "dp")),
            P(("groups", "dp")),
        ),
        out_specs=P(("groups", "dp"), None),
        check_vma=False,
    )
```

```python
import functools

import jax
import jax.numpy as jnp
from jax import lax
from jax.experimental import pallas as pl
from jax.experimental.pallas import tpu as pltpu
from jax.sharding import PartitionSpec as P

BLK = 8
SLOTS = 2
LANE = 128
ROW_TILE = 16
LOADS = 4
CROSS = 3
STAY = 1
MESH = pl.DeviceIdType.MESH


def dp_at(pos, n):
    back = pos // (n // 2)
    return (1 - back) * (2 * pos) + back * (2 * (n - 1 - pos) + 1)


def place_of(dev, n):
    odd = dev % 2
    return (1 - odd) * (dev // 2) + odd * (n - 1 - dev // 2)


def padded(rows, n):
    spill = max((rows * d) % LANE for d in range(n))
    return -(-(rows + spill) // LANE) * LANE


def cuts(first, size, parts):
    ends = [first + size * i // parts for i in range(parts + 1)]
    return [(low, high - low) for low, high in zip(ends, ends[1:])]


def start_and_shift(dev, rows, span, total, n):
    offset = dev * rows
    start = offset - offset % LANE
    if any(rows * d - (rows * d) % LANE + span > total for d in range(n)):
        start = jnp.minimum(start, total - span)
    return pl.multiple_of(start, LANE), offset - start


def kernel(
    n, acts_hbm, grads_hbm, basis_in_hbm, basis_out_hbm, owner_hbm, slot_hbm, fill_hbm, out_ref,
    acts, grads, basis_in, basis_out, owner, slot, fill, shards, acc_in, acc_out, part, other_part,
    turned, message, arrived, tally, tally_in, half, other_half,
    load_sem, small_sem, ring_send, ring_recv, x_send, x_recv, mp_send, mp_recv, rs_send, rs_recv,
    tally_send, tally_recv,
):
    group, me, core = lax.axis_index("groups"), lax.axis_index("dp"), lax.axis_index("mp")
    tokens = acts.shape[0]
    width, rows_in = basis_in.shape
    rows_out = basis_out.shape[1]
    span_in, span_out = padded(rows_in, n), padded(rows_out, n)
    steps = n // 2
    pos = place_of(me, n)
    right = dp_at((pos + 1) % n, n)
    left = dp_at((pos + n - 1) % n, n)
    mate = group + 1 - 2 * (group % 2)
    twin = 1 - core
    to_mate = {"groups": mate}
    to_twin = {"mp": twin}

    barrier = pltpu.get_barrier_semaphore()
    for device in ({"dp": right}, {"dp": left}, to_mate, to_twin):
        pl.semaphore_signal(barrier, inc=1, device_id=device, device_id_type=MESH)

    smalls = [
        pltpu.make_async_copy(source, target, small_sem.at[i])
        for i, (source, target) in enumerate(
            [(basis_out_hbm, basis_out), (basis_in_hbm, basis_in), (owner_hbm, owner),
             (slot_hbm, slot), (fill_hbm, fill)]
        )
    ]
    for copy in smalls:
        copy.start()
    loads = [pltpu.make_async_copy(acts_hbm, acts, load_sem.at[LOADS])]
    slab = tokens // LOADS
    for i in range(LOADS):
        at = pl.ds(i * slab, slab)
        loads.append(pltpu.make_async_copy(grads_hbm.at[at], grads.at[at], load_sem.at[i]))
    def aligned(basis, span, total):
        rows = basis.shape[1]
        _, shift = start_and_shift(me, rows, span, total, n)
        wide = jnp.concatenate(
            [basis[...].astype(jnp.float32), jnp.zeros((width, span - rows), jnp.float32)], axis=1
        )
        return pltpu.roll(wide, shift, 1).astype(jnp.bfloat16)

    for copy in smalls[:2]:
        copy.wait()
    share = jnp.concatenate(
        [aligned(basis_in, span_in, acts.shape[1]), aligned(basis_out, span_out, grads.shape[1])], axis=1
    )
    tiles, tiles_in = share.shape[1] // LANE, span_in // LANE
    for i in range(tiles):
        shards[me, i] = share[:, i * LANE : (i + 1) * LANE]
    pl.semaphore_wait(barrier, 4)

    third = max(2, tiles * 3 // 8)
    cross = cuts(0, third, CROSS)
    stay = cuts(2 * third, tiles - 2 * third, STAY)
    mine_at, mate_at = (group % 2) * third, (1 - group % 2) * third

    def piece_of(from_dev, base, piece, step, way):
        first, size = piece
        if step < steps:
            return shards.at[from_dev, pl.ds(base + first, size)]
        return shards.at[from_dev, pl.ds(base + first, size), pl.ds(way * (width // 2), width // 2)]

    def origin(step, way):
        return dp_at((pos + n - step) % n if way == 0 else (pos + step) % n, n)

    def ring_copy(step, way, piece, from_dev):
        base, part_of = (mine_at, cross[piece]) if piece < CROSS else (0, stay[piece - CROSS])
        ref = piece_of(from_dev, base, part_of, step, way)
        return pltpu.make_async_remote_copy(
            src_ref=ref, dst_ref=ref,
            send_sem=ring_send.at[way, step - 1, piece],
            recv_sem=ring_recv.at[way, step - 1, piece],
            device_id={"dp": right if way == 0 else left}, device_id_type=MESH,
        )

    def x_copy(step, way, piece, base):
        ref = piece_of(origin(step, way), base, cross[piece], step, way)
        return pltpu.make_async_remote_copy(
            src_ref=ref, dst_ref=ref,
            send_sem=x_send.at[way, step - 1, piece], recv_sem=x_recv.at[way, step - 1, piece],
            device_id=to_mate, device_id_type=MESH,
        )

    def from_mate(step):
        for way in range(2):
            for piece in range(CROSS):
                x_copy(step, way, piece, mate_at).wait_recv()

    sent = []

    def send(copy):
        copy.start()
        sent.append(copy)

    for piece in range(CROSS + STAY):
        for way in range(2):
            send(ring_copy(1, way, piece, me))
    for load in loads:
        load.start()
    acc_in[...] = jnp.zeros_like(acc_in)
    acc_out[...] = jnp.zeros_like(acc_out)
    across = (((1,), (1,)), ((), ()))

    def features_of(dev, first, end):
        return jnp.concatenate([shards[dev, i] for i in range(first, end)], axis=1)

    def multiply(dev):
        start_in, _ = start_and_shift(dev, rows_in, span_in, acts.shape[1], n)
        start_out, _ = start_and_shift(dev, rows_out, span_out, grads.shape[1], n)
        acc_in[...] += lax.dot_general(
            acts[:, pl.ds(start_in, span_in)], features_of(dev, 0, tiles_in),
            across, preferred_element_type=jnp.float32,
        )
        acc_out[...] += lax.dot_general(
            grads[:, pl.ds(start_out, span_out)], features_of(dev, tiles_in, tiles),
            across, preferred_element_type=jnp.float32,
        )

    def multiply_both(step):
        def body(way, carry):
            multiply(dp_at((pos + (1 - way) * (n - step) + way * step) % n, n))
            return carry
        lax.fori_loop(0, 2, body, 0)

    for copy in smalls[2:]:
        copy.wait()
    blocks = owner.shape[1]
    examples = n * SLOTS
    example = (owner[...] * SLOTS + slot[...]).astype(jnp.float32)
    facts = jnp.concatenate(
        [jnp.broadcast_to(example, (8, blocks)), jnp.broadcast_to(fill[...].astype(jnp.float32), (8, blocks))],
        axis=0,
    ).astype(jnp.bfloat16)
    token_at = lax.broadcasted_iota(jnp.int32, (blocks, tokens), 1)
    spread = (token_at // BLK == lax.broadcasted_iota(jnp.int32, (blocks, tokens), 0)).astype(jnp.float32)
    by_token = jnp.dot(facts, spread.astype(jnp.bfloat16), preferred_element_type=jnp.float32)
    place = lax.broadcasted_iota(jnp.int32, (1, tokens), 1) % BLK
    live = place.astype(jnp.float32) < by_token[8:9, :]
    number = lax.broadcasted_iota(jnp.int32, (examples, tokens), 0).astype(jnp.float32)
    weight = jnp.where((number == by_token[0:1, :]) & live, 1.0, 0.0)
    count = jnp.broadcast_to(jnp.sum(weight, axis=1, keepdims=True), (examples, LANE))
    for d in range(n):
        tally[d] = jnp.concatenate(
            [jnp.broadcast_to(count[d * SLOTS + s : d * SLOTS + s + 1, :], (8, LANE)) for s in range(SLOTS)],
            axis=0,
        ).astype(jnp.bfloat16)

    def tally_copy(step, way, slot_at):
        peer = origin(step, 1 - way)
        return pltpu.make_async_remote_copy(
            src_ref=tally.at[peer], dst_ref=tally_in.at[slot_at],
            send_sem=tally_send.at[way, step - 1], recv_sem=tally_recv.at[way, step - 1],
            device_id={"dp": peer}, device_id_type=MESH,
        )

    def pass_on(step, pieces):
        for piece in pieces:
            for way in range(2):
                from_dev = origin(step, way)
                ring_copy(step, way, piece, from_dev).wait_recv()
                if piece < CROSS:
                    send(x_copy(step, way, piece, mine_at))
                if step < steps:
                    send(ring_copy(step + 1, way, piece, from_dev))

    for step in range(1, steps + 1):
        pass_on(step, range(CROSS))
        if step > 2:
            from_mate(step - 2)
            multiply_both(step - 2)
        pass_on(step, range(CROSS, CROSS + STAY))
        for way in range(2 if step < steps else 1):
            send(tally_copy(step, way, me))
        if step == 1:
            for load in loads:
                load.wait()
            multiply(me)
    from_mate(steps - 1)

    def finish(i, carry):
        pl.when(i == 2)(lambda: from_mate(steps))
        far = dp_at((pos + steps) % n, n)
        near = dp_at((pos + (1 - i % 2) * (n - steps + 1) + (i % 2) * (steps - 1)) % n, n)
        multiply((i // 2) * far + (1 - i // 2) * near)
        return carry

    lax.fori_loop(0, 3, finish, 0)

    lane = lax.broadcasted_iota(jnp.int32, (tokens, LANE), 1)
    part[...] = jnp.concatenate([acc_in[...], acc_out[...]], axis=1)
    swap = pltpu.make_async_remote_copy(
        src_ref=part, dst_ref=other_part, send_sem=mp_send.at[0], recv_sem=mp_recv.at[0],
        device_id=to_twin, device_id_type=MESH,
    )
    swap.start()
    swap.wait()
    total = part[...] + other_part[...]
    outs = jnp.where(lane < width, pltpu.roll(total, width, 1), total).astype(jnp.bfloat16)
    flipped = jnp.transpose(total)[:width, :]
    quarter = width // 4
    lots = tokens // LANE
    for b in range(lots):
        turned[pl.ds(b * width, width), :] = flipped[:, b * LANE : (b + 1) * LANE]

    def features(first):
        at = core * (width // 2) + first
        return jnp.concatenate(
            [turned[pl.ds(b * width + at, quarter, stride=2), :] for b in range(lots)], axis=1
        )

    evens, odds = features(0), features(1)
    masked = [(evens * weight[e : e + 1, :]).astype(jnp.bfloat16) for e in range(examples)]
    masked += [(odds * weight[e : e + 1, :]).astype(jnp.bfloat16) for e in range(examples)]
    outer = jnp.dot(jnp.concatenate(masked, axis=0), outs, preferred_element_type=jnp.float32)
    size = examples * quarter
    lane_out = lax.broadcasted_iota(jnp.int32, (size, LANE), 1)
    outer = jnp.where(lane_out < width, outer[:size], outer[size:]).astype(jnp.bfloat16)
    data = SLOTS * quarter
    for d in range(n):
        message[d] = outer[d * data : (d + 1) * data]

    def route(k, slot_at):
        peer = (me + k) % n
        return pltpu.make_async_remote_copy(
            src_ref=message.at[peer], dst_ref=arrived.at[slot_at],
            send_sem=rs_send.at[k - 1], recv_sem=rs_recv.at[k - 1],
            device_id={"dp": peer}, device_id_type=MESH,
        )

    gather_sent = list(sent)
    sent.clear()
    for k in range(1, n):
        send(route(k, me))
    for copy in gather_sent:
        copy.wait_send()
    counted = tally[me].astype(jnp.float32)
    for step in range(1, steps + 1):
        for way in range(2 if step < steps else 1):
            source = origin(step, way)
            tally_copy(step, way, source).wait_recv()
            counted = counted + tally_in[source].astype(jnp.float32)
    scale = jnp.concatenate([
        jnp.broadcast_to(jnp.sqrt(jnp.maximum(counted[8 * s : 8 * s + 1, :], 1.0)), (quarter, LANE))
        for s in range(SLOTS)
    ], axis=0)
    summed = message[me].astype(jnp.float32)
    for k in range(1, n):
        source = (me + n - k) % n
        route(k, source).wait_recv()
        summed = summed + arrived[source].astype(jnp.float32)
    half[...] = summed / scale
    last = pltpu.make_async_remote_copy(
        src_ref=half, dst_ref=other_half, send_sem=mp_send.at[1], recv_sem=mp_recv.at[1],
        device_id=to_twin, device_id_type=MESH,
    )
    last.start()
    for copy in sent:
        copy.wait_send()
    last.wait()
    for s in range(SLOTS):
        at = pl.ds(s * quarter, quarter)
        out_ref[s, pl.ds(pl.multiple_of(core * quarter, 8), quarter), :] = half[at, :]
        out_ref[s, pl.ds(pl.multiple_of(twin * quarter, 8), quarter), :] = other_half[at, :]


def local(acts, grads_out, basis_in, basis_out, owner, slot, fill):
    n = lax.axis_size("dp")
    tokens = acts.shape[0]
    width = basis_in.shape[1]
    steps = n // 2
    span = padded(basis_in.shape[0], n) + padded(basis_out.shape[0], n)
    quarter = width // 4
    message_rows = SLOTS * quarter
    f32, bf16, i32 = jnp.float32, jnp.bfloat16, jnp.int32
    hbm = pl.BlockSpec(memory_space=pltpu.HBM)
    dma = pltpu.SemaphoreType.DMA
    blocks = (1, owner.shape[0])
    result = pl.pallas_call(
        functools.partial(kernel, n),
        out_shape=jax.ShapeDtypeStruct((SLOTS, width // 2, LANE), f32),
        in_specs=[hbm] * 7,
        out_specs=pl.BlockSpec(memory_space=pltpu.VMEM),
        scratch_shapes=[
            pltpu.VMEM(acts.shape, bf16),
            pltpu.VMEM(grads_out.shape, bf16),
            pltpu.VMEM(basis_in.shape[::-1], bf16),
            pltpu.VMEM(basis_out.shape[::-1], bf16),
            pltpu.VMEM(blocks, i32),
            pltpu.VMEM(blocks, i32),
            pltpu.VMEM(blocks, i32),
            pltpu.VMEM((n, span // LANE, width, LANE), bf16),
            pltpu.VMEM((tokens, width), f32),
            pltpu.VMEM((tokens, width), f32),
            pltpu.VMEM((tokens, LANE), f32),
            pltpu.VMEM((tokens, LANE), f32),
            pltpu.VMEM((width * (tokens // LANE), LANE), f32),
            pltpu.VMEM((n, message_rows, LANE), bf16),
            pltpu.VMEM((n, message_rows, LANE), bf16),
            pltpu.VMEM((n, 8 * SLOTS, LANE), bf16),
            pltpu.VMEM((n, 8 * SLOTS, LANE), bf16),
            pltpu.VMEM((SLOTS * quarter, LANE), f32),
            pltpu.VMEM((SLOTS * quarter, LANE), f32),
            dma((LOADS + 1,)),
            dma((5,)),
            dma((2, steps, CROSS + STAY)),
            dma((2, steps, CROSS + STAY)),
            dma((2, steps, CROSS)),
            dma((2, steps, CROSS)),
            dma((2,)),
            dma((2,)),
            dma((n - 1,)),
            dma((n - 1,)),
            dma((2, steps)),
            dma((2, steps)),
        ],
        compiler_params=pltpu.CompilerParams(
            collective_id=0, has_side_effects=True, vmem_limit_bytes=63 * 1024 * 1024
        ),
    )(acts, grads_out, basis_in.T, basis_out.T, owner.T, slot[None, :], fill[None, :])
    return result.reshape(SLOTS, width * width)


def solution(mesh):
    return jax.shard_map(
        local,
        mesh=mesh,
        in_specs=(
            P(("groups", "dp"), "mp"),
            P(("groups", "dp"), "mp"),
            P(("mp", "dp"), None),
            P(("mp", "dp"), None),
            P(("groups", "dp"), None),
            P(("groups", "dp")),
            P(("groups", "dp")),
        ),
        out_specs=P(("groups", "dp"), None),
        check_vma=False,
    )
```

```python
import functools

import jax
import jax.numpy as jnp
from jax import lax
from jax.experimental import pallas as pl
from jax.experimental.pallas import tpu as pltpu
from jax.sharding import PartitionSpec as P

BLK = 8
SLOTS = 2
LANE = 128
ROW_TILE = 16
LOADS = 4
CROSS = 3
STAY = 1
MESH = pl.DeviceIdType.MESH


def dp_at(pos, n):
    back = pos // (n // 2)
    return (1 - back) * (2 * pos) + back * (2 * (n - 1 - pos) + 1)


def place_of(dev, n):
    odd = dev % 2
    return (1 - odd) * (dev // 2) + odd * (n - 1 - dev // 2)


def padded(rows, n):
    spill = max((rows * d) % LANE for d in range(n))
    return -(-(rows + spill) // LANE) * LANE


def cuts(first, size, parts):
    ends = [first + size * i // parts for i in range(parts + 1)]
    return [(low, high - low) for low, high in zip(ends, ends[1:])]


def start_and_shift(dev, rows, span, total, n):
    offset = dev * rows
    start = offset - offset % LANE
    if any(rows * d - (rows * d) % LANE + span > total for d in range(n)):
        start = jnp.minimum(start, total - span)
    return pl.multiple_of(start, LANE), offset - start


def kernel(
    n, acts_hbm, grads_hbm, basis_in_hbm, basis_out_hbm, owner_hbm, slot_hbm, fill_hbm, out_ref,
    acts, grads, basis_in, basis_out, owner, slot, fill, shards, acc_in, acc_out, part, other_part,
    turned, message, arrived, tally, tally_in, half, other_half,
    load_sem, small_sem, ring_send, ring_recv, x_send, x_recv, mp_send, mp_recv, rs_send, rs_recv,
    tally_send, tally_recv,
):
    group, me, core = lax.axis_index("groups"), lax.axis_index("dp"), lax.axis_index("mp")
    tokens = acts.shape[0]
    width, rows_in = basis_in.shape
    rows_out = basis_out.shape[1]
    span_in, span_out = padded(rows_in, n), padded(rows_out, n)
    steps = n // 2
    pos = place_of(me, n)
    right = dp_at((pos + 1) % n, n)
    left = dp_at((pos + n - 1) % n, n)
    mate = group + 1 - 2 * (group % 2)
    twin = 1 - core
    to_mate = {"groups": mate}
    to_twin = {"mp": twin}

    barrier = pltpu.get_barrier_semaphore()
    for device in ({"dp": right}, {"dp": left}, to_mate, to_twin):
        pl.semaphore_signal(barrier, inc=1, device_id=device, device_id_type=MESH)

    smalls = [
        pltpu.make_async_copy(source, target, small_sem.at[i])
        for i, (source, target) in enumerate(
            [(basis_out_hbm, basis_out), (basis_in_hbm, basis_in), (owner_hbm, owner),
             (slot_hbm, slot), (fill_hbm, fill)]
        )
    ]
    for copy in smalls:
        copy.start()
    loads = [pltpu.make_async_copy(acts_hbm, acts, load_sem.at[LOADS])]
    slab = tokens // LOADS
    for i in range(LOADS):
        at = pl.ds(i * slab, slab)
        loads.append(pltpu.make_async_copy(grads_hbm.at[at], grads.at[at], load_sem.at[i]))
    def aligned(basis, span, total):
        rows = basis.shape[1]
        _, shift = start_and_shift(me, rows, span, total, n)
        wide = jnp.concatenate(
            [basis[...].astype(jnp.float32), jnp.zeros((width, span - rows), jnp.float32)], axis=1
        )
        return pltpu.roll(wide, shift, 1).astype(jnp.bfloat16)

    for copy in smalls[:2]:
        copy.wait()
    share = jnp.concatenate(
        [aligned(basis_in, span_in, acts.shape[1]), aligned(basis_out, span_out, grads.shape[1])], axis=1
    )
    tiles, tiles_in = share.shape[1] // LANE, span_in // LANE
    for i in range(tiles):
        shards[me, i] = share[:, i * LANE : (i + 1) * LANE]
    pl.semaphore_wait(barrier, 4)

    third = max(2, tiles * 3 // 8)
    cross = cuts(0, third, CROSS)
    stay = cuts(2 * third, tiles - 2 * third, STAY)
    mine_at, mate_at = (group % 2) * third, (1 - group % 2) * third

    def piece_of(from_dev, base, piece, step, way):
        first, size = piece
        if step < steps:
            return shards.at[from_dev, pl.ds(base + first, size)]
        return shards.at[from_dev, pl.ds(base + first, size), pl.ds(way * (width // 2), width // 2)]

    def origin(step, way):
        return dp_at((pos + n - step) % n if way == 0 else (pos + step) % n, n)

    def ring_copy(step, way, piece, from_dev):
        base, part_of = (mine_at, cross[piece]) if piece < CROSS else (0, stay[piece - CROSS])
        ref = piece_of(from_dev, base, part_of, step, way)
        return pltpu.make_async_remote_copy(
            src_ref=ref, dst_ref=ref,
            send_sem=ring_send.at[way, step - 1, piece],
            recv_sem=ring_recv.at[way, step - 1, piece],
            device_id={"dp": right if way == 0 else left}, device_id_type=MESH,
        )

    def x_copy(step, way, piece, base):
        ref = piece_of(origin(step, way), base, cross[piece], step, way)
        return pltpu.make_async_remote_copy(
            src_ref=ref, dst_ref=ref,
            send_sem=x_send.at[way, step - 1, piece], recv_sem=x_recv.at[way, step - 1, piece],
            device_id=to_mate, device_id_type=MESH,
        )

    def from_mate(step):
        for way in range(2):
            for piece in range(CROSS):
                x_copy(step, way, piece, mate_at).wait_recv()

    sent = []

    def send(copy):
        copy.start()
        sent.append(copy)

    for piece in range(CROSS + STAY):
        for way in range(2):
            send(ring_copy(1, way, piece, me))
    for load in loads:
        load.start()
    acc_in[...] = jnp.zeros_like(acc_in)
    acc_out[...] = jnp.zeros_like(acc_out)
    across = (((1,), (1,)), ((), ()))

    def features_of(dev, first, end):
        return jnp.concatenate([shards[dev, i] for i in range(first, end)], axis=1)

    def multiply(dev):
        start_in, _ = start_and_shift(dev, rows_in, span_in, acts.shape[1], n)
        start_out, _ = start_and_shift(dev, rows_out, span_out, grads.shape[1], n)
        acc_in[...] += lax.dot_general(
            acts[:, pl.ds(start_in, span_in)], features_of(dev, 0, tiles_in),
            across, preferred_element_type=jnp.float32,
        )
        acc_out[...] += lax.dot_general(
            grads[:, pl.ds(start_out, span_out)], features_of(dev, tiles_in, tiles),
            across, preferred_element_type=jnp.float32,
        )

    def multiply_both(step):
        def body(way, carry):
            multiply(dp_at((pos + (1 - way) * (n - step) + way * step) % n, n))
            return carry
        lax.fori_loop(0, 2, body, 0)

    for copy in smalls[2:]:
        copy.wait()
    blocks = owner.shape[1]
    examples = n * SLOTS
    example = (owner[...] * SLOTS + slot[...]).astype(jnp.float32)
    facts = jnp.concatenate(
        [jnp.broadcast_to(example, (8, blocks)), jnp.broadcast_to(fill[...].astype(jnp.float32), (8, blocks))],
        axis=0,
    ).astype(jnp.bfloat16)
    token_at = lax.broadcasted_iota(jnp.int32, (blocks, tokens), 1)
    spread = (token_at // BLK == lax.broadcasted_iota(jnp.int32, (blocks, tokens), 0)).astype(jnp.float32)
    by_token = jnp.dot(facts, spread.astype(jnp.bfloat16), preferred_element_type=jnp.float32)
    place = lax.broadcasted_iota(jnp.int32, (1, tokens), 1) % BLK
    live = place.astype(jnp.float32) < by_token[8:9, :]
    number = lax.broadcasted_iota(jnp.int32, (examples, tokens), 0).astype(jnp.float32)
    weight = jnp.where((number == by_token[0:1, :]) & live, 1.0, 0.0)
    count = jnp.broadcast_to(jnp.sum(weight, axis=1, keepdims=True), (examples, LANE))
    for d in range(n):
        tally[d] = jnp.concatenate(
            [jnp.broadcast_to(count[d * SLOTS + s : d * SLOTS + s + 1, :], (8, LANE)) for s in range(SLOTS)],
            axis=0,
        ).astype(jnp.bfloat16)

    def tally_copy(step, way, slot_at):
        peer = origin(step, 1 - way)
        return pltpu.make_async_remote_copy(
            src_ref=tally.at[peer], dst_ref=tally_in.at[slot_at],
            send_sem=tally_send.at[way, step - 1], recv_sem=tally_recv.at[way, step - 1],
            device_id={"dp": peer}, device_id_type=MESH,
        )

    def pass_on(step, pieces):
        for piece in pieces:
            for way in range(2):
                from_dev = origin(step, way)
                ring_copy(step, way, piece, from_dev).wait_recv()
                if piece < CROSS:
                    send(x_copy(step, way, piece, mine_at))
                if step < steps:
                    send(ring_copy(step + 1, way, piece, from_dev))

    for step in range(1, steps + 1):
        pass_on(step, range(CROSS))
        if step > 2:
            from_mate(step - 2)
            multiply_both(step - 2)
        pass_on(step, range(CROSS, CROSS + STAY))
        for way in range(2 if step < steps else 1):
            send(tally_copy(step, way, me))
        if step == 1:
            for load in loads:
                load.wait()
            multiply(me)
    from_mate(steps - 1)

    def finish(i, carry):
        pl.when(i == 2)(lambda: from_mate(steps))
        far = dp_at((pos + steps) % n, n)
        near = dp_at((pos + (1 - i % 2) * (n - steps + 1) + (i % 2) * (steps - 1)) % n, n)
        multiply((i // 2) * far + (1 - i // 2) * near)
        return carry

    lax.fori_loop(0, 3, finish, 0)

    lane = lax.broadcasted_iota(jnp.int32, (tokens, LANE), 1)
    part[...] = jnp.concatenate([acc_in[...], acc_out[...]], axis=1)
    swap = pltpu.make_async_remote_copy(
        src_ref=part, dst_ref=other_part, send_sem=mp_send.at[0], recv_sem=mp_recv.at[0],
        device_id=to_twin, device_id_type=MESH,
    )
    swap.start()
    swap.wait_recv()
    sent.append(swap)
    total = part[...] + other_part[...]
    outs = jnp.where(lane < width, pltpu.roll(total, width, 1), total).astype(jnp.bfloat16)
    flipped = jnp.transpose(total)[:width, :]
    quarter = width // 4
    lots = tokens // LANE
    for b in range(lots):
        turned[pl.ds(b * width, width), :] = flipped[:, b * LANE : (b + 1) * LANE]

    def features(first):
        at = core * (width // 2) + first
        return jnp.concatenate(
            [turned[pl.ds(b * width + at, quarter, stride=2), :] for b in range(lots)], axis=1
        )

    evens, odds = features(0), features(1)
    masked = [(evens * weight[e : e + 1, :]).astype(jnp.bfloat16) for e in range(examples)]
    masked += [(odds * weight[e : e + 1, :]).astype(jnp.bfloat16) for e in range(examples)]
    outer = jnp.dot(jnp.concatenate(masked, axis=0), outs, preferred_element_type=jnp.float32)
    size = examples * quarter
    lane_out = lax.broadcasted_iota(jnp.int32, (size, LANE), 1)
    outer = jnp.where(lane_out < width, outer[:size], outer[size:]).astype(jnp.bfloat16)
    data = SLOTS * quarter
    for d in range(n):
        message[d] = outer[d * data : (d + 1) * data]

    def route(k, slot_at):
        peer = (me + k) % n
        return pltpu.make_async_remote_copy(
            src_ref=message.at[peer], dst_ref=arrived.at[slot_at],
            send_sem=rs_send.at[k - 1], recv_sem=rs_recv.at[k - 1],
            device_id={"dp": peer}, device_id_type=MESH,
        )

    gather_sent = list(sent)
    sent.clear()
    for k in range(1, n):
        send(route(k, me))
    for copy in gather_sent:
        copy.wait_send()
    counted = tally[me].astype(jnp.float32)
    for step in range(1, steps + 1):
        for way in range(2 if step < steps else 1):
            source = origin(step, way)
            tally_copy(step, way, source).wait_recv()
            counted = counted + tally_in[source].astype(jnp.float32)
    scale = jnp.concatenate([
        jnp.broadcast_to(jnp.sqrt(jnp.maximum(counted[8 * s : 8 * s + 1, :], 1.0)), (quarter, LANE))
        for s in range(SLOTS)
    ], axis=0)
    summed = message[me].astype(jnp.float32)
    for k in range(1, n):
        source = (me + n - k) % n
        route(k, source).wait_recv()
        summed = summed + arrived[source].astype(jnp.float32)
    half[...] = summed / scale
    last = pltpu.make_async_remote_copy(
        src_ref=half, dst_ref=other_half, send_sem=mp_send.at[1], recv_sem=mp_recv.at[1],
        device_id=to_twin, device_id_type=MESH,
    )
    last.start()
    last.wait_recv()
    for s in range(SLOTS):
        at = pl.ds(s * quarter, quarter)
        out_ref[s, pl.ds(pl.multiple_of(core * quarter, 8), quarter), :] = half[at, :]
        out_ref[s, pl.ds(pl.multiple_of(twin * quarter, 8), quarter), :] = other_half[at, :]
    for copy in sent + [last]:
        copy.wait_send()


def local(acts, grads_out, basis_in, basis_out, owner, slot, fill):
    n = lax.axis_size("dp")
    tokens = acts.shape[0]
    width = basis_in.shape[1]
    steps = n // 2
    span = padded(basis_in.shape[0], n) + padded(basis_out.shape[0], n)
    quarter = width // 4
    message_rows = SLOTS * quarter
    f32, bf16, i32 = jnp.float32, jnp.bfloat16, jnp.int32
    hbm = pl.BlockSpec(memory_space=pltpu.HBM)
    dma = pltpu.SemaphoreType.DMA
    blocks = (1, owner.shape[0])
    result = pl.pallas_call(
        functools.partial(kernel, n),
        out_shape=jax.ShapeDtypeStruct((SLOTS, width // 2, LANE), f32),
        in_specs=[hbm] * 7,
        out_specs=pl.BlockSpec(memory_space=pltpu.VMEM),
        scratch_shapes=[
            pltpu.VMEM(acts.shape, bf16),
            pltpu.VMEM(grads_out.shape, bf16),
            pltpu.VMEM(basis_in.shape[::-1], bf16),
            pltpu.VMEM(basis_out.shape[::-1], bf16),
            pltpu.VMEM(blocks, i32),
            pltpu.VMEM(blocks, i32),
            pltpu.VMEM(blocks, i32),
            pltpu.VMEM((n, span // LANE, width, LANE), bf16),
            pltpu.VMEM((tokens, width), f32),
            pltpu.VMEM((tokens, width), f32),
            pltpu.VMEM((tokens, LANE), f32),
            pltpu.VMEM((tokens, LANE), f32),
            pltpu.VMEM((width * (tokens // LANE), LANE), f32),
            pltpu.VMEM((n, message_rows, LANE), bf16),
            pltpu.VMEM((n, message_rows, LANE), bf16),
            pltpu.VMEM((n, 8 * SLOTS, LANE), bf16),
            pltpu.VMEM((n, 8 * SLOTS, LANE), bf16),
            pltpu.VMEM((SLOTS * quarter, LANE), f32),
            pltpu.VMEM((SLOTS * quarter, LANE), f32),
            dma((LOADS + 1,)),
            dma((5,)),
            dma((2, steps, CROSS + STAY)),
            dma((2, steps, CROSS + STAY)),
            dma((2, steps, CROSS)),
            dma((2, steps, CROSS)),
            dma((2,)),
            dma((2,)),
            dma((n - 1,)),
            dma((n - 1,)),
            dma((2, steps)),
            dma((2, steps)),
        ],
        compiler_params=pltpu.CompilerParams(
            collective_id=0, has_side_effects=True, vmem_limit_bytes=63 * 1024 * 1024
        ),
    )(acts, grads_out, basis_in.T, basis_out.T, owner.T, slot[None, :], fill[None, :])
    return result.reshape(SLOTS, width * width)


def solution(mesh):
    return jax.shard_map(
        local,
        mesh=mesh,
        in_specs=(
            P(("groups", "dp"), "mp"),
            P(("groups", "dp"), "mp"),
            P(("mp", "dp"), None),
            P(("mp", "dp"), None),
            P(("groups", "dp"), None),
            P(("groups", "dp")),
            P(("groups", "dp")),
        ),
        out_specs=P(("groups", "dp"), None),
        check_vma=False,
    )
```
